32 devices in a mesh: seq: 8 (over z, y), exp: 4 (over x, core).
Axes of the slice: x: 2, y: 2, z: 4, core: 2. Of those that a mesh axis runs over, the one named last changes fastest.
Arguments:
- qkv_input: bfloat16 [4096, 16, 512], P('seq', 'exp'), may hold values from -6 to 6
- z_gate: bfloat16 [4096, 4096], P('seq', 'exp'), may hold values from -6 to 6
- beta_logit: float32 [4096, 32], P('seq', 'exp'), may hold values from -6 to 6
- decay_input: float32 [4096, 32], P('seq', 'exp'), may hold values from -8 to 8
- decay_rate: float32 [32], P('exp'), may hold values from 1.2207031e-05 to 0.06
- conv_weight: float32 [4, 16, 512], P(None, 'exp'), may hold values from -3 to 3
- cache_state: float32 [8, 32, 128, 128], P('seq', 'exp'), may hold values from -4 to 4
- cache_tail: float32 [8, 3, 16, 512], P('seq', None, 'exp'), may hold values from -6 to 6
- block_request: int32 [64], replicated, may hold values from 0 to 7, never falling along the last dimension, each value on 1 to 32 neighbouring positions
- cache_owner: int32 [8], replicated, may hold values from 0 to 7, each once
- norm_gain: float32 [128], replicated, may hold values from 0.1 to 1.9
- out_weight: bfloat16 [4096, 2048], P('exp'), may hold values from -0.09375 to 0.09375
- residual: bfloat16 [4096, 2048], P(('seq', 'exp')), may hold values from -6 to 6
- post_gain: float32 [2048], replicated, may hold values from 0.1 to 1.9
- expert_ids: int32 [4096, 10], P(('seq', 'exp')), may hold values from 0 to 31, all different within a row; in each aligned block of 128 rows (0 to 127, 128 to 255, ...) at most 48 rows name the same one
- expert_weights: float32 [4096, 10], P(('seq', 'exp')), may hold values from 0.1 to 1
- expert_gate: bfloat16 [32, 2048, 512], P(('seq', 'exp')), may hold values from -0.125 to 0.125
- expert_up: bfloat16 [32, 2048, 512], P(('seq', 'exp')), may hold values from -0.125 to 0.125
- expert_down: bfloat16 [32, 512, 2048], P(('seq', 'exp')), may hold values from -0.25 to 0.25
Outputs:
- layer_out: bfloat16 [4096, 2048], P(('seq', 'exp'))
The draws below stay inside these ranges and needn't reach their ends.
Inputs may be any that keep to these rules, and one draw needn't show every extreme that they name: Block c belongs to request block_request[c]; requests are numbered in order, each covers 1 to 32 whole blocks, and one covers exactly 32. `cache_owner`: each cache slot belongs to exactly one request. `expert_ids`: the 10 experts of a row differ; in the 128 rows of one device no expert is named more than 48 times, a bound that some block reaches.
All inputs are finite; a program needn't handle non-finite values.
Results may differ from the reference program's by a relative error of at most 0.013.
Values may be sent and summed in bfloat16 or wider, within the bound.
A program may use at most 128 MiB of HBM per device.

```python
import math
import jax
import jax.numpy as jnp
import numpy as np
from jax import lax

D = 2048
HEAD = 128
KHEADS = 16
VHEADS = 32
GROUP = 2
CONV = 4
FFN = 512
TOP = 10
BLOCK = 64
TOK_DEV = 128
TOKENS = 4096
NCHUNK = 64
REQS = 8
EXPERTS = 32
CAP = 48
N_SEQ = 8
N_EXP = 4


def draw_decay_rate(key, part):
    pick_key, slow_key, fast_key = jax.random.split(key, 3)
    keep_share = 0.5
    slow_mask = jax.random.uniform(pick_key, (VHEADS,), dtype=jnp.float32) < keep_share
    slow_rates = jnp.exp(jax.random.uniform(slow_key, (VHEADS,), dtype=jnp.float32, minval=math.log(0.05 / TOKENS), maxval=math.log(1.0 / TOKENS)))
    fast_rates = jnp.exp(jax.random.uniform(fast_key, (VHEADS,), dtype=jnp.float32, minval=math.log(0.02), maxval=math.log(0.06)))
    return jnp.where(slow_mask, slow_rates, fast_rates).astype(jnp.float32)


def level_of(stream_key, shape, pieces, smallest, top_value):
    gain, own = 1.0, jax.random.fold_in(stream_key, 6)
    for dim, shards_of in pieces:
        heights = jnp.exp(jax.random.uniform(jax.random.fold_in(own, dim), (shards_of,), jnp.float32, smallest / len(pieces), top_value / len(pieces)))
        gain = gain * jnp.repeat(heights, shape[dim] // shards_of).reshape([-1 if axis == dim else 1 for axis in range(len(shape))])
    return gain


def profile(number_of, total, limit, lean):
    portions = [(1 << 20) // math.isqrt(grade ** lean) + 1 for grade in range(2, number_of + 1)]
    rest, counts = total - limit - (number_of - 1), [1] * (number_of - 1)
    while rest > 0:
        candidates = [i for i in range(number_of - 1) if counts[i] < limit]
        mass, left = sum([portions[i] for i in candidates]), rest
        for i in candidates:
            extra = min(limit - counts[i], max(1, left * portions[i] // mass), rest)
            counts[i] = counts[i] + extra
            rest = rest - extra
    return np.array([limit] + counts)


def uneven(key, amount, total, most, skew):
    if amount == 2:
        one = jax.random.randint(key, (), max(1, total - most), min(most, total - 1) + 1)
        return jnp.stack([one, total - one])
    tallies = jnp.asarray(profile(amount, total, most, skew), jnp.int32)
    pairs = (amount - 1) // 2
    source_of, sink = tallies[1:1 + 2 * pairs:2], tallies[2:2 + 2 * pairs:2]
    margin = jnp.minimum(source_of - 1, most - sink)
    shifted = jax.random.randint(jax.random.fold_in(key, 1), (pairs,), 0, 1 << 20) % (margin + 1)
    tallies = tallies.at[1:1 + 2 * pairs:2].set(source_of - shifted).at[2:2 + 2 * pairs:2].set(sink + shifted)
    return tallies[jax.random.permutation(jax.random.fold_in(key, 2), amount)]


def shared_out(own_key, own, number, rows, count, top, limit, skew):
    sequence = jax.random.permutation(own_key, count)
    heavy_load, ordinary = load_shares(count, rows * top, limit, skew, True), load_shares(count, rows * top, limit, skew, False)
    places = jnp.arange(count)

    def named(sizes, offset_by):
        used = int((sizes > 0).sum())
        fixed = max(1, used // 4)
        moved = fixed + (places - fixed + offset_by * (used - fixed)) % max(1, count - fixed)
        return jnp.zeros((count,), jnp.int32).at[sequence[jnp.where(places < fixed, places, moved)]].set(jnp.asarray(sizes, jnp.int32))

    sizes = jnp.where(number % 4 == 0, named(heavy_load, number // 4), named(ordinary, number - number // 4 - 1))
    mixed = jax.random.permutation(jax.random.fold_in(own, 3), count)
    giver, taker = mixed[0:count // 2 * 2:2], mixed[1:count // 2 * 2:2]
    room = jnp.minimum(sizes[giver] - 1, limit - sizes[taker]) // 2
    room = jnp.where((giver == sequence[0]) | (taker == sequence[0]) | (sizes[taker] == 0), 0, jnp.maximum(room, 0))
    moved = jax.random.randint(jax.random.fold_in(own, 4), (count // 2,), 0, 1 << 20) % (room + 1)
    sizes = sizes.at[giver].add(-moved).at[taker].add(moved)
    members = jnp.searchsorted(jnp.cumsum(sizes), jnp.arange(rows * top), side="right").astype(jnp.int32)
    grid = members.reshape(top, rows).T
    grid = grid[jax.random.permutation(jax.random.fold_in(own, 1), rows)]
    offset_by = jax.random.randint(jax.random.fold_in(own, 2), (rows, 1), 0, top)
    return jnp.take_along_axis(grid, (jnp.arange(top)[None, :] + offset_by) % top, axis=1)


def load_shares(amount, total, reach, slope, full):
    portions = [(1 << 20) // math.isqrt(standing ** slope) + 1 for standing in range(1, amount + 1)]
    largest = reach if full else min(reach, max(-(-total // amount), total * portions[0] // sum(portions)))
    least = 1 if total - largest >= amount - 1 else 0
    holding, surplus = [largest] + [least] * (amount - 1), total - largest - least * (amount - 1)
    while surplus > 0:
        candidates = [i for i in range(1, amount) if holding[i] < largest] or [i for i in range(1, amount) if holding[i] < reach]
        mass, remaining = sum([portions[i] for i in candidates]), surplus
        for i in candidates:
            more = min(reach - holding[i], max(1, remaining * portions[i] // mass), surplus)
            holding[i] = holding[i] + more
            surplus = surplus - more
    return np.array(holding)


def bell_draw(rng, dims, scale, bound, cuts=(), held_as=jnp.bfloat16):
    array = jax.random.normal(rng, dims, jnp.float32) * scale
    if len(cuts) > 0:
        array = level_of(rng, dims, cuts, -0.22, 0.18) * array
    return jnp.clip(array, min=-bound, max=bound).astype(held_as)


def setup_inputs(seed: int = 0) -> dict:
    splits = jax.random.split(jax.random.key(seed), 20)
    qkv_input = bell_draw(splits[0], (TOKENS, KHEADS, (2 + GROUP) * HEAD), 1.0, 6.0, ((0, 8), (1, 4)))
    z_gate = bell_draw(splits[1], (TOKENS, VHEADS * HEAD), 1.0, 6.0, ((0, 8), (1, 4)))
    beta_logit = bell_draw(splits[2], (TOKENS, VHEADS), 1.5, 6.0, ((0, 8), (1, 4)), jnp.float32)
    decay_input = bell_draw(splits[3], (TOKENS, VHEADS), 2.0, 8.0, ((0, 8), (1, 4)), jnp.float32)
    decay_rate = draw_decay_rate(jax.random.fold_in(splits[19], 71), 0)
    conv_weight = bell_draw(splits[5], (CONV, KHEADS, (2 + GROUP) * HEAD), CONV ** -0.5, 3.0, ((1, 4),), jnp.float32)
    cache_state = bell_draw(splits[6], (REQS, VHEADS, HEAD, HEAD), 0.5, 4.0, ((0, 8), (1, 4)), jnp.float32)
    cache_tail = bell_draw(splits[7], (REQS, CONV - 1, KHEADS, (2 + GROUP) * HEAD), 1.0, 6.0, ((0, 8), (2, 4)), jnp.float32)
    block_request = jnp.searchsorted(jnp.cumsum(uneven(splits[8], REQS, NCHUNK, NCHUNK // 2, 2)), jnp.arange(NCHUNK), side="right").astype(jnp.int32)
    cache_owner = jax.random.permutation(splits[9], REQS).astype(jnp.int32)
    norm_gain = jnp.clip(1.0 + 0.18 * jax.random.normal(splits[10], (HEAD,), jnp.float32), 0.1, 1.9)
    out_weight = bell_draw(splits[11], (VHEADS * HEAD, D), (VHEADS * HEAD) ** -0.5, 0.09375, ((0, 4),))
    residual = bell_draw(splits[12], (TOKENS, D), 1.0, 6.0, ((0, 32),))
    post_gain = jnp.clip(1.0 + 0.18 * jax.random.normal(splits[13], (D,), jnp.float32), 0.1, 1.9)
    expert_ids_keys = jax.random.split(jax.random.fold_in(splits[14], 1), TOKENS // TOK_DEV)
    expert_ids_turns = jax.random.permutation(jax.random.fold_in(splits[14], 3), TOKENS // TOK_DEV)
    expert_ids = jax.vmap(lambda own, number: shared_out(jax.random.fold_in(splits[14], 2), own, number, TOK_DEV, EXPERTS, TOP, CAP, 2))(expert_ids_keys, expert_ids_turns).reshape((TOKENS, TOP))
    expert_weights = jnp.clip(0.1 + 0.9 * jax.random.uniform(splits[15], (TOKENS, TOP), jnp.float32) ** level_of(splits[15], (TOKENS, TOP), ((0, 32),), -0.2, 0.2), 0.1, 1.0)
    expert_gate = bell_draw(splits[16], (EXPERTS, D, FFN), D ** -0.5, 0.125, ((0, 32),))
    expert_up = bell_draw(splits[17], (EXPERTS, D, FFN), D ** -0.5, 0.125, ((0, 32),))
    expert_down = bell_draw(splits[18], (EXPERTS, FFN, D), FFN ** -0.5, 0.25, ((0, 32),))
    return dict(qkv_input=qkv_input, z_gate=z_gate, beta_logit=beta_logit, decay_input=decay_input, decay_rate=decay_rate, conv_weight=conv_weight, cache_state=cache_state, cache_tail=cache_tail, block_request=block_request, cache_owner=cache_owner, norm_gain=norm_gain, out_weight=out_weight, residual=residual, post_gain=post_gain, expert_ids=expert_ids, expert_weights=expert_weights, expert_gate=expert_gate, expert_up=expert_up, expert_down=expert_down)


precise = lax.Precision.HIGHEST

def chain_product(left, right):
    return jnp.einsum('...ik,...kj->...ij', left, right, precision=precise)

def head_split(convolved):
    length = convolved.shape[0]
    group_count = convolved.shape[1]
    query_rows = convolved[..., :HEAD]
    key_rows = convolved[..., HEAD:2 * HEAD]
    value_rows = convolved[..., 2 * HEAD:].reshape(length, group_count * GROUP, HEAD)
    query_rows = query_rows * lax.rsqrt(lax.optimization_barrier(jnp.sum(query_rows * query_rows, axis=-1, keepdims=True)) + 1e-06) / math.sqrt(HEAD)
    key_rows = key_rows * lax.rsqrt(lax.optimization_barrier(jnp.sum(key_rows * key_rows, axis=-1, keepdims=True)) + 1e-06)
    query_rows = jnp.repeat(query_rows, GROUP, axis=1)
    key_rows = jnp.repeat(key_rows, GROUP, axis=1)
    return (query_rows, key_rows, value_rows)

def block_parts(query_rows, key_rows, value_rows, beta, log_decay):
    row_width = key_rows.shape[-1]
    span = log_decay.shape[-1]
    running = jnp.cumsum(log_decay, axis=-1)
    later = jnp.arange(span)[:, None]
    earlier = jnp.arange(span)[None, :]
    inclusive = later >= earlier
    spread = running[..., :, None] - running[..., None, :]
    decay_mat = jnp.where(inclusive, jnp.exp(jnp.where(inclusive, spread, 0.0)), 0.0)
    strict_mat = jnp.where(later > earlier, decay_mat, 0.0)
    key_key = jnp.einsum('...id,...jd->...ij', key_rows, key_rows, precision=precise)
    lower_mat = beta[..., :, None] * key_key * strict_mat + jnp.eye(span, dtype=jnp.float32)
    growth = jnp.exp(running)
    right_side = jnp.concatenate([(beta * growth)[..., None] * key_rows, beta[..., None] * value_rows], axis=-1)
    solved = lax.linalg.triangular_solve(lower_mat, right_side, left_side=True, lower=True, unit_diagonal=True)
    weighted_keys = solved[..., :row_width]
    new_values = solved[..., row_width:]
    carried_keys = jnp.exp(running[..., -1:] - running)[..., None] * key_rows
    query_key = jnp.einsum('...id,...jd->...ij', query_rows, key_rows, precision=precise) * decay_mat
    return (growth, weighted_keys, new_values, carried_keys, query_key)

def block_out(parts, query_rows, start_state):
    growth, weighted_keys, new_values, carried_keys, query_key = parts
    fixed_values = new_values - chain_product(weighted_keys, start_state)
    output = growth[..., None] * chain_product(query_rows, start_state)
    output = output + chain_product(query_key, fixed_values)
    return (output, fixed_values)

def gate_norm(core, z_gate, norm_gain):
    scaled = core * lax.rsqrt(lax.optimization_barrier(jnp.mean(core * core, axis=-1, keepdims=True)) + 1e-06) * norm_gain
    return (scaled.reshape(z_gate.shape) * jax.nn.silu(z_gate.astype(jnp.float32))).astype(jnp.bfloat16)

def reference(qkv_input, z_gate, beta_logit, decay_input, decay_rate, conv_weight, cache_state, cache_tail, block_request, cache_owner, norm_gain, out_weight, residual, post_gain, expert_ids, expert_weights, expert_gate, expert_up, expert_down):
    previous = jnp.concatenate([jnp.full((1,), -1, jnp.int32), block_request[:-1]])
    starts_all = block_request != previous
    padded = jnp.concatenate([jnp.zeros((CONV - 1,) + qkv_input.shape[1:], qkv_input.dtype), qkv_input], axis=0)
    beta_all = jax.nn.sigmoid(beta_logit)
    decay_all = -decay_rate[None, :] * jax.nn.softplus(decay_input)
    tails = cache_tail[cache_owner]
    cached = cache_state[cache_owner]

    def advance(state, block):
        request = block_request[block]
        is_first = starts_all[block]
        first_row = (block * BLOCK).astype(jnp.int32)
        window = lax.dynamic_slice_in_dim(padded, first_row, BLOCK + CONV - 1, 0).astype(jnp.float32)
        before = jnp.where(is_first, tails[request], window[:CONV - 1])
        window = jnp.concatenate([before, window[CONV - 1:]], axis=0)
        convolved = sum((conv_weight[offset] * window[offset:offset + BLOCK] for offset in range(CONV)))
        convolved = jax.nn.silu(convolved)
        query_rows, key_rows, value_rows = head_split(convolved)
        query_rows = query_rows.transpose(1, 0, 2)
        key_rows = key_rows.transpose(1, 0, 2)
        value_rows = value_rows.transpose(1, 0, 2)
        beta = lax.dynamic_slice_in_dim(beta_all, first_row, BLOCK, 0).T
        log_decay = lax.dynamic_slice_in_dim(decay_all, first_row, BLOCK, 0).T
        start_state = jnp.where(is_first, cached[request], state)
        parts = block_parts(query_rows, key_rows, value_rows, beta, log_decay)
        output, fixed_values = block_out(parts, query_rows, start_state)
        growth = parts[0]
        carried_keys = parts[3]
        end_state = growth[..., -1, None, None] * start_state + jnp.einsum('...ik,...ij->...kj', carried_keys, fixed_values, precision=precise)
        return (end_state, output)
    initial = jnp.zeros((VHEADS, HEAD, HEAD), jnp.float32)
    _, outputs = lax.scan(advance, initial, jnp.arange(NCHUNK, dtype=jnp.int32))
    core = outputs.transpose(0, 2, 1, 3).reshape(TOKENS, VHEADS, HEAD)
    gated = gate_norm(core, z_gate, norm_gain)
    columns = VHEADS * HEAD // N_EXP
    attn = jnp.zeros((TOKENS, D), jnp.float32)
    for group in range(N_EXP):
        partial_sum = jnp.dot(gated[:, group * columns:(group + 1) * columns].astype(jnp.float32), out_weight[group * columns:(group + 1) * columns].astype(jnp.float32), preferred_element_type=jnp.float32)
        attn = attn + lax.optimization_barrier(partial_sum.astype(jnp.bfloat16)).astype(jnp.float32)
    mid = (residual.astype(jnp.float32) + attn).astype(jnp.bfloat16)
    mid_wide = mid.astype(jnp.float32)
    normed = (mid_wide * lax.rsqrt(lax.optimization_barrier(jnp.mean(mid_wide * mid_wide, axis=-1, keepdims=True)) + 1e-06) * post_gain).astype(jnp.bfloat16)
    route = expert_weights / lax.optimization_barrier(jnp.sum(expert_weights, axis=-1, keepdims=True))
    flat_ids = expert_ids.reshape(-1)
    flat_route = route.reshape(-1)
    order = jnp.argsort(flat_ids, stable=True).astype(jnp.int32)
    sorted_ids = flat_ids[order]
    expert_range = jnp.arange(EXPERTS, dtype=jnp.int32)
    first_pick = jnp.searchsorted(sorted_ids, expert_range).astype(jnp.int32)
    last_pick = jnp.searchsorted(sorted_ids, expert_range, side='right').astype(jnp.int32)
    span = N_SEQ * N_EXP * CAP
    order = jnp.concatenate([order, jnp.zeros((span,), jnp.int32)])

    def expert_step(total, expert):
        picks = lax.dynamic_slice_in_dim(order, first_pick[expert], span, 0)
        valid = jnp.arange(span) < last_pick[expert] - first_pick[expert]
        tokens_at = picks // TOP
        rows_in = normed[tokens_at]
        gate_part = jnp.dot(rows_in.astype(jnp.float32), expert_gate[expert].astype(jnp.float32), preferred_element_type=jnp.float32)
        up_part = jnp.dot(rows_in.astype(jnp.float32), expert_up[expert].astype(jnp.float32), preferred_element_type=jnp.float32)
        hidden = (jax.nn.silu(gate_part) * up_part).astype(jnp.bfloat16)
        result = jnp.dot(hidden.astype(jnp.float32), expert_down[expert].astype(jnp.float32), preferred_element_type=jnp.float32).astype(jnp.bfloat16)
        weight = jnp.where(valid, flat_route[picks], 0.0)
        total = total.at[tokens_at].add(weight[:, None] * result.astype(jnp.float32))
        return (total, None)
    moe_sum, _ = lax.scan(expert_step, jnp.zeros((TOKENS, D), jnp.float32), expert_range)
    return (mid_wide + moe_sum).astype(jnp.bfloat16)
```

```python
import math

import jax
import jax.numpy as jnp
from jax import lax
from jax.experimental import pallas as pl
from jax.experimental.pallas import tpu as pltpu
from jax.sharding import PartitionSpec as P

D = 2048
HEAD = 128
GROUP = 2
CONV = 4
BLOCK = 64


PACK = 4
LANES = PACK * BLOCK
VMEM_LIMIT = 56 * 1024 * 1024


def product(left, right, contract):
    return lax.dot_general(left, right, (contract, ((), ())), preferred_element_type=jnp.float32)


def split(value):
    high = value.astype(jnp.bfloat16)
    return (high, (value - high.astype(jnp.float32)).astype(jnp.bfloat16))


def fine(left, right, contract=((1,), (0,))):
    left_high, left_low = split(left)
    right_high, right_low = split(right)
    return (
        product(left_high, right_high, contract)
        + product(left_high, right_low, contract)
        + product(left_low, right_high, contract)
    )


def coarse(left, right, contract=((1,), (0,))):
    return product(left.astype(jnp.bfloat16), right.astype(jnp.bfloat16), contract)


def silu(value):
    return value / (1.0 + jnp.exp(-value))


def parts_kernel(
    x_ref, before_ref, taps_ref, col_ref, row_ref, query_ref, key_ref, weighted_ref, values_ref, mix_ref, ext
):
    ext[0:8, :] = before_ref[0]
    ext[8:, :] = x_ref[...].astype(jnp.float32)
    row_id = lax.broadcasted_iota(jnp.int32, (LANES, LANES), 0)
    col_id = lax.broadcasted_iota(jnp.int32, (LANES, LANES), 1)
    same_head = row_id // BLOCK == col_id // BLOCK
    inclusive = same_head & (row_id >= col_id)
    strict = same_head & (row_id > col_id)
    group_width = (2 + GROUP) * HEAD
    heads = col_ref.shape[1] // BLOCK
    for pack in range(heads // PACK):
        queries, keys, values = [], [], []
        for group in range(PACK // GROUP):
            first = (pack * (PACK // GROUP) + group) * group_width
            columns = slice(first, first + group_width)
            mixed = ext[5 : 5 + BLOCK, columns] * taps_ref[0:1, columns]
            for tap in range(1, CONV):
                mixed = mixed + ext[5 + tap : 5 + tap + BLOCK, columns] * taps_ref[tap : tap + 1, columns]
            mixed = silu(mixed)
            query = mixed[:, :HEAD]
            query = query * (
                lax.rsqrt(jnp.sum(query * query, axis=1, keepdims=True) + 1e-06) / math.sqrt(HEAD)
            )
            key = mixed[:, HEAD : 2 * HEAD]
            key = key * lax.rsqrt(jnp.sum(key * key, axis=1, keepdims=True) + 1e-06)
            queries += [query, query]
            keys += [key, key]
            values += [mixed[:, 2 * HEAD : 3 * HEAD], mixed[:, 3 * HEAD :]]
        query = jnp.concatenate(queries, axis=0)
        key = jnp.concatenate(keys, axis=0)
        value = jnp.concatenate(values, axis=0)
        rows = slice(pack * LANES, (pack + 1) * LANES)
        col = col_ref[0, rows, :]
        running, beta, growth, tail = col[:, 0:1], col[:, 1:2], col[:, 2:3], col[:, 3:4]
        decay = jnp.where(
            inclusive, jnp.exp(jnp.where(inclusive, running - row_ref[0, pack : pack + 1, :], 0.0)), 0.0
        )
        across = ((1,), (1,))
        lower = jnp.where(strict, beta * fine(key, key, across) * decay, 0.0)
        mix_ref[0, rows, :] = (coarse(query, key, across) * decay).astype(jnp.bfloat16)
        inverse = jnp.where(row_id == col_id, 1.0, 0.0) - jnp.where(
            row_id // 2 == col_id // 2, lower, 0.0
        )
        size = 2
        while size < BLOCK:
            joint = (row_id // (2 * size) == col_id // (2 * size)) & (row_id // size != col_id // size)
            between = jnp.where(joint, lower, 0.0)
            inverse = inverse - fine(fine(inverse, between), inverse)
            size *= 2
        solved = fine(
            inverse, jnp.concatenate([(beta * growth) * key, beta * value], axis=1)
        )
        query_ref[0, rows, :] = (growth * query).astype(jnp.bfloat16)
        key_ref[0, rows, :] = tail * key
        weighted_ref[0, rows, :] = solved[:, :HEAD]
        values_ref[0, rows, :] = solved[:, HEAD:]


def maps_kernel(first_ref, slot_ref, key_ref, weighted_ref, values_ref, col_ref, cache_ref, out_ref, total):
    block = pl.program_id(0)
    heads = total.shape[0]

    @pl.when(block == 0)
    def _():
        eye = jnp.where(
            lax.broadcasted_iota(jnp.int32, (HEAD, HEAD), 0)
            == lax.broadcasted_iota(jnp.int32, (HEAD, HEAD), 1),
            1.0,
            0.0,
        )
        for head in range(heads):
            total[head] = jnp.concatenate([eye, jnp.zeros((HEAD, HEAD), jnp.float32)], axis=1)

    @pl.when(first_ref[block] == 1)
    def _():
        for head in range(heads):
            total[head] = jnp.concatenate(
                [jnp.zeros((HEAD, HEAD), jnp.float32), cache_ref[0, head].astype(jnp.float32)], axis=1
            )

    for head in range(heads):
        rows = slice(head * BLOCK, (head + 1) * BLOCK)
        state = total[head]
        fixed = (
            jnp.concatenate([jnp.zeros((BLOCK, HEAD), jnp.float32), values_ref[0, rows, :]], axis=1)
            - fine(weighted_ref[0, rows, :], state)
        )
        last = col_ref[0, head * BLOCK : head * BLOCK + 1, 4:5]
        total[head] = last * state + fine(key_ref[0, rows, :], fixed, ((0,), (0,)))

    @pl.when(block == pl.num_programs(0) - 1)
    def _():
        out_ref[...] = total[...].astype(jnp.bfloat16)


def advance_kernel(
    first_ref, slot_ref, place_ref,
    maps_ref, query_ref, key_ref, weighted_ref, values_ref, mix_ref, col_ref, cache_ref, z_ref, gain_ref,
    out_ref, total,
):
    block = pl.program_id(0)
    heads = total.shape[0]

    @pl.when(block == 0)
    def _():
        total[...] = jnp.zeros_like(total)

        def one(step, carry):
            for head in range(heads):
                both = maps_ref[step, head]
                state_high, state_low = split(total[head])
                transfer = both[:, :HEAD]
                contract = ((1,), (0,))
                total[head] = (
                    product(transfer, state_high, contract)
                    + product(transfer, state_low, contract)
                    + both[:, HEAD:].astype(jnp.float32)
                )
            return carry

        lax.fori_loop(0, place_ref[0], one, 0)

    @pl.when(first_ref[block] == 1)
    def _():
        for head in range(heads):
            total[head] = cache_ref[0, head].astype(jnp.float32)

    for pack in range(heads // PACK):
        fixed_rows, outputs = [], []
        for inner in range(PACK):
            head = pack * PACK + inner
            rows = slice(head * BLOCK, (head + 1) * BLOCK)
            state = total[head]
            fixed = values_ref[0, rows, :] - fine(weighted_ref[0, rows, :], state)
            outputs.append(product(query_ref[0, rows, :], state.astype(jnp.bfloat16), ((1,), (0,))))
            last = col_ref[0, head * BLOCK : head * BLOCK + 1, 4:5]
            total[head] = last * state + fine(key_ref[0, rows, :], fixed, ((0,), (0,)))
            fixed_rows.append(fixed.astype(jnp.bfloat16))
        rows = slice(pack * LANES, (pack + 1) * LANES)
        core = jnp.concatenate(outputs, axis=0) + product(
            mix_ref[0, rows, :], jnp.concatenate(fixed_rows, axis=0), ((1,), (0,))
        )
        core = core * lax.rsqrt(jnp.mean(core * core, axis=1, keepdims=True) + 1e-06) * gain_ref[...]
        for inner in range(PACK):
            columns = slice((pack * PACK + inner) * HEAD, (pack * PACK + inner + 1) * HEAD)
            gate = silu(z_ref[:, columns].astype(jnp.float32))
            out_ref[:, columns] = (core[inner * BLOCK : (inner + 1) * BLOCK] * gate).astype(jnp.bfloat16)


def expert_apply(arrived, expert_gate, expert_up, expert_down):
    flat_rows = arrived.reshape(-1, D)
    gate_part = jnp.dot(flat_rows, expert_gate[0], preferred_element_type=jnp.float32)
    up_part = jnp.dot(flat_rows, expert_up[0], preferred_element_type=jnp.float32)
    hidden = (jax.nn.silu(gate_part) * up_part).astype(jnp.bfloat16)
    result = jnp.dot(hidden, expert_down[0], preferred_element_type=jnp.float32).astype(
        jnp.bfloat16
    )
    return result.reshape(arrived.shape)


def local(
    qkv_input,
    z_gate,
    beta_logit,
    decay_input,
    decay_rate,
    conv_weight,
    cache_state,
    cache_tail,
    block_request,
    cache_owner,
    norm_gain,
    out_weight,
    residual,
    post_gain,
    expert_ids,
    expert_weights,
    expert_gate,
    expert_up,
    expert_down,
):
    seq_len, key_heads, row_width = qkv_input.shape
    blocks = seq_len // BLOCK
    head_count = z_gate.shape[1] // HEAD
    seq_count = lax.axis_size("seq")
    exp_count = lax.axis_size("exp")
    previous = jnp.concatenate([jnp.full((1,), -1, jnp.int32), block_request[:-1]])
    starts_all = block_request != previous
    first_block = lax.axis_index("seq") * blocks
    local_request = lax.dynamic_slice_in_dim(block_request, first_block, blocks, 0)
    local_start = lax.dynamic_slice_in_dim(starts_all, first_block, blocks, 0)
    request_ids = jnp.arange(cache_owner.shape[0], dtype=jnp.int32)
    local_slot = jnp.sum(
        jnp.where(local_request[:, None] == request_ids[None, :], cache_owner[None, :], 0), axis=1
    )
    states_all = lax.all_gather(cache_state.astype(jnp.bfloat16), "seq", axis=0, tiled=True)
    width = key_heads * row_width
    rows_flat = qkv_input.reshape(seq_len, width)
    edge = jnp.concatenate(
        [
            cache_tail.astype(jnp.bfloat16).reshape(-1, width),
            rows_flat[seq_len - (CONV - 1) :],
        ],
        axis=0,
    )
    edges = lax.all_gather(edge, "seq", axis=0)
    tails_all = edges[:, : -(CONV - 1)].reshape(-1, CONV - 1, width)
    place = lax.axis_index("seq")
    rim_rows = lax.dynamic_index_in_dim(
        edges[:, -(CONV - 1) :], jnp.maximum(place - 1, 0), 0, False
    )
    before = jnp.concatenate(
        [rim_rows[None], rows_flat.reshape(blocks, BLOCK, width)[:-1, BLOCK - (CONV - 1) :]], axis=0
    )
    before = jnp.where(local_start[:, None, None], tails_all[local_slot], before)
    before = jnp.pad(before.astype(jnp.float32), ((0, 0), (8 - (CONV - 1), 0), (0, 0)))
    beta = jax.nn.sigmoid(beta_logit).reshape(blocks, BLOCK, head_count).transpose(0, 2, 1)
    log_decay = (
        (-decay_rate[None, :] * jax.nn.softplus(decay_input))
        .reshape(blocks, BLOCK, head_count)
        .transpose(0, 2, 1)
    )
    running = jnp.cumsum(log_decay, axis=-1)
    last = running[..., -1:]
    grown = jnp.exp(last)
    columns = jnp.stack(
        [running, beta, jnp.exp(running), jnp.exp(last - running)]
        + [jnp.broadcast_to(grown, running.shape)] * 4,
        axis=-1,
    ).reshape(blocks, head_count * BLOCK, 8)
    packs = head_count // PACK
    running_rows = running.reshape(blocks, packs, LANES)
    stacked = head_count * BLOCK
    rows_spec = pl.BlockSpec((1, stacked, HEAD), lambda b, *_: (b, 0, 0))
    mix_spec = pl.BlockSpec((1, stacked, LANES), lambda b, *_: (b, 0, 0))
    col_spec = pl.BlockSpec((1, stacked, 8), lambda b, *_: (b, 0, 0))
    cache_spec = pl.BlockSpec(
        (1, head_count, HEAD, HEAD), lambda b, first, slot, *_: (slot[b], 0, 0, 0)
    )
    params = pltpu.CompilerParams(vmem_limit_bytes=VMEM_LIMIT)
    rows_shape = (blocks, stacked, HEAD)
    queries, carried, weighted, new_values, mix = pl.pallas_call(
        parts_kernel,
        grid=(blocks,),
        in_specs=[
            pl.BlockSpec((BLOCK, width), lambda b: (b, 0)),
            pl.BlockSpec((1, 8, width), lambda b: (b, 0, 0)),
            pl.BlockSpec((CONV, width), lambda b: (0, 0)),
            col_spec,
            pl.BlockSpec((1, packs, LANES), lambda b: (b, 0, 0)),
        ],
        out_specs=[rows_spec] * 4 + [mix_spec],
        out_shape=[
            jax.ShapeDtypeStruct(rows_shape, jnp.bfloat16),
            jax.ShapeDtypeStruct(rows_shape, jnp.float32),
            jax.ShapeDtypeStruct(rows_shape, jnp.float32),
            jax.ShapeDtypeStruct(rows_shape, jnp.float32),
            jax.ShapeDtypeStruct((blocks, stacked, LANES), jnp.bfloat16),
        ],
        scratch_shapes=[pltpu.VMEM((8 + BLOCK, width), jnp.float32)],
        compiler_params=params,
        cost_estimate=pl.CostEstimate(
            flops=blocks * packs * 40 * 2 * LANES**3, bytes_accessed=16 * 2**20, transcendentals=0
        ),
    )(rows_flat, before, conv_weight.reshape(CONV, width), columns, running_rows)
    firsts = local_start.astype(jnp.int32)
    own_map = pl.pallas_call(
        maps_kernel,
        grid_spec=pltpu.PrefetchScalarGridSpec(
            num_scalar_prefetch=2,
            grid=(blocks,),
            in_specs=[rows_spec, rows_spec, rows_spec, col_spec, cache_spec],
            out_specs=pl.BlockSpec((head_count, HEAD, 2 * HEAD), lambda b, *_: (0, 0, 0)),
            scratch_shapes=[pltpu.VMEM((head_count, HEAD, 2 * HEAD), jnp.float32)],
        ),
        out_shape=jax.ShapeDtypeStruct((head_count, HEAD, 2 * HEAD), jnp.bfloat16),
        compiler_params=params,
    )(firsts, local_slot, carried, weighted, new_values, columns, states_all)
    maps_all = lax.all_gather(own_map, "seq")
    gated = pl.pallas_call(
        advance_kernel,
        grid_spec=pltpu.PrefetchScalarGridSpec(
            num_scalar_prefetch=3,
            grid=(blocks,),
            in_specs=[
                pl.BlockSpec(maps_all.shape, lambda b, *_: (0, 0, 0, 0), pipeline_mode=pl.Buffered(1)),
                rows_spec,
                rows_spec,
                rows_spec,
                rows_spec,
                mix_spec,
                col_spec,
                cache_spec,
                pl.BlockSpec((BLOCK, head_count * HEAD), lambda b, *_: (b, 0)),
                pl.BlockSpec((1, HEAD), lambda b, *_: (0, 0)),
            ],
            out_specs=pl.BlockSpec((BLOCK, head_count * HEAD), lambda b, *_: (b, 0)),
            scratch_shapes=[pltpu.VMEM((head_count, HEAD, HEAD), jnp.float32)],
        ),
        out_shape=jax.ShapeDtypeStruct(z_gate.shape, jnp.bfloat16),
        compiler_params=params,
    )(
        firsts, local_slot, place.reshape(1),
        maps_all, queries, carried, weighted, new_values, mix, columns, states_all, z_gate, norm_gain[None],
    )
    rows_in = gated
    attn = lax.psum_scatter(
        jnp.dot(rows_in, out_weight, preferred_element_type=jnp.float32).astype(jnp.bfloat16),
        "exp",
        scatter_dimension=0,
        tiled=True,
    ).astype(jnp.float32)
    mid_wide = (residual.astype(jnp.float32) + attn).astype(jnp.bfloat16).astype(jnp.float32)
    normed = (
        mid_wide
        * lax.rsqrt(jnp.mean(mid_wide * mid_wide, axis=-1, keepdims=True) + 1e-06)
        * post_gain
    ).astype(jnp.bfloat16)
    route = expert_weights / jnp.sum(expert_weights, axis=-1, keepdims=True)
    token_count, top_count = expert_ids.shape
    expert_count = seq_count * exp_count
    capacity = max(2, token_count * top_count * 6 // (expert_count * 5))
    names = jnp.arange(expert_count, dtype=expert_ids.dtype)
    chosen = expert_ids[:, :, None] == names
    hot = jnp.any(chosen, axis=1)
    share = jnp.sum(jnp.where(chosen, route[:, :, None], 0.0), axis=1)
    rank = jnp.cumsum(hot.astype(jnp.int32), axis=0) - 1
    placed = hot[:, :, None] & (rank[:, :, None] == jnp.arange(capacity, dtype=jnp.int32))
    flat_placed = placed.astype(jnp.bfloat16).reshape(token_count, expert_count * capacity)
    outgoing = jnp.dot(flat_placed.T, normed, preferred_element_type=jnp.float32).astype(jnp.bfloat16)
    devices = ("seq", "exp")
    arrived = lax.all_to_all(outgoing, devices, split_axis=0, concat_axis=0, tiled=True)
    results = expert_apply(arrived, expert_gate, expert_up, expert_down)
    returned = lax.all_to_all(results, devices, split_axis=0, concat_axis=0, tiled=True)
    share_high, share_low = split(share)
    moe_sum = sum(
        jnp.dot(
            (placed * part[:, :, None]).reshape(token_count, expert_count * capacity),
            returned,
            preferred_element_type=jnp.float32,
        )
        for part in (share_high, share_low)
    )
    return (mid_wide + moe_sum).astype(jnp.bfloat16)


def solution(mesh):
    in_specs = (
        P("seq", "exp", None),
        P("seq", "exp"),
        P("seq", "exp"),
        P("seq", "exp"),
        P("exp"),
        P(None, "exp", None),
        P("seq", "exp", None, None),
        P("seq", None, "exp", None),
        P(),
        P(),
        P(),
        P("exp", None),
        P(("seq", "exp"), None),
        P(),
        P(("seq", "exp"), None),
        P(("seq", "exp"), None),
        P(("seq", "exp"), None, None),
        P(("seq", "exp"), None, None),
        P(("seq", "exp"), None, None),
    )
    out_specs = P(("seq", "exp"), None)
    return jax.shard_map(local, mesh=mesh, in_specs=in_specs, out_specs=out_specs, check_vma=False)
```

```python
import math

import jax
import jax.numpy as jnp
from jax import lax
from jax.experimental import pallas as pl
from jax.experimental.pallas import tpu as pltpu
from jax.sharding import PartitionSpec as P

D = 2048
HEAD = 128
GROUP = 2
CONV = 4
BLOCK = 64


PACK = 2
LANES = PACK * BLOCK
VMEM_LIMIT = 56 * 1024 * 1024


def product(left, right, contract):
    return lax.dot_general(left, right, (contract, ((), ())), preferred_element_type=jnp.float32)


def split(value):
    high = value.astype(jnp.bfloat16)
    return (high, (value - high.astype(jnp.float32)).astype(jnp.bfloat16))


def fine(left, right, contract=((1,), (0,))):
    left_high, left_low = split(left)
    right_high, right_low = split(right)
    return (
        product(left_high, right_high, contract)
        + product(left_high, right_low, contract)
        + product(left_low, right_high, contract)
    )


def coarse(left, right, contract=((1,), (0,))):
    return product(left.astype(jnp.bfloat16), right.astype(jnp.bfloat16), contract)


def silu(value):
    return value / (1.0 + jnp.exp(-value))


def parts_kernel(
    x_ref, before_ref, taps_ref, row_ref, query_ref, key_ref, weighted_ref, values_ref, mix_ref, ext
):
    ext[0:8, :] = before_ref[0]
    ext[8:, :] = x_ref[...].astype(jnp.float32)
    row_id = lax.broadcasted_iota(jnp.int32, (LANES, LANES), 0)
    col_id = lax.broadcasted_iota(jnp.int32, (LANES, LANES), 1)
    same_head = row_id // BLOCK == col_id // BLOCK
    inclusive = same_head & (row_id >= col_id)
    strict = same_head & (row_id > col_id)
    group_width = (2 + GROUP) * HEAD
    heads = row_ref.shape[2] // BLOCK
    cols = row_ref[0].T
    for pack in range(heads // PACK):
        queries, keys, values = [], [], []
        for group in range(PACK // GROUP):
            first = (pack * (PACK // GROUP) + group) * group_width
            columns = slice(first, first + group_width)
            mixed = ext[5 : 5 + BLOCK, columns] * taps_ref[0:1, columns]
            for tap in range(1, CONV):
                mixed = mixed + ext[5 + tap : 5 + tap + BLOCK, columns] * taps_ref[tap : tap + 1, columns]
            mixed = silu(mixed)
            query = mixed[:, :HEAD]
            query = query * (
                lax.rsqrt(jnp.sum(query * query, axis=1, keepdims=True) + 1e-06) / math.sqrt(HEAD)
            )
            key = mixed[:, HEAD : 2 * HEAD]
            key = key * lax.rsqrt(jnp.sum(key * key, axis=1, keepdims=True) + 1e-06)
            queries += [query, query]
            keys += [key, key]
            values += [mixed[:, 2 * HEAD : 3 * HEAD], mixed[:, 3 * HEAD :]]
        query = jnp.concatenate(queries, axis=0)
        key = jnp.concatenate(keys, axis=0)
        value = jnp.concatenate(values, axis=0)
        rows = slice(pack * LANES, (pack + 1) * LANES)
        col = cols[rows, :]
        running, beta, growth, tail = col[:, 0:1], col[:, 1:2], col[:, 2:3], col[:, 3:4]
        decay = jnp.where(
            inclusive, jnp.exp(jnp.where(inclusive, running - row_ref[0, 0:1, rows], 0.0)), 0.0
        )
        across = ((1,), (1,))
        lower = jnp.where(strict, beta * fine(key, key, across) * decay, 0.0)
        mix_ref[0, rows, :] = (coarse(query, key, across) * decay).astype(jnp.bfloat16)
        inverse = jnp.where(row_id == col_id, 1.0, 0.0) - jnp.where(
            row_id // 2 == col_id // 2, lower, 0.0
        )
        size = 2
        while size < BLOCK:
            joint = (row_id // (2 * size) == col_id // (2 * size)) & (row_id // size != col_id // size)
            between = jnp.where(joint, lower, 0.0)
            inverse = inverse - fine(fine(inverse, between), inverse)
            size *= 2
        solved = fine(
            inverse, jnp.concatenate([(beta * growth) * key, beta * value], axis=1)
        )
        query_ref[0, rows, :] = (growth * query).astype(jnp.bfloat16)
        key_ref[0, rows, :] = tail * key
        weighted_ref[0, rows, :] = solved[:, :HEAD]
        values_ref[0, rows, :] = solved[:, HEAD:]


def maps_kernel(first_ref, slot_ref, key_ref, weighted_ref, values_ref, col_ref, cache_ref, out_ref, total):
    block = pl.program_id(0)
    heads = total.shape[0]

    @pl.when(block == 0)
    def _():
        eye = jnp.where(
            lax.broadcasted_iota(jnp.int32, (HEAD, HEAD), 0)
            == lax.broadcasted_iota(jnp.int32, (HEAD, HEAD), 1),
            1.0,
            0.0,
        )
        for head in range(heads):
            total[head] = jnp.concatenate([eye, jnp.zeros((HEAD, HEAD), jnp.float32)], axis=1)

    @pl.when(first_ref[block] == 1)
    def _():
        for head in range(heads):
            total[head] = jnp.concatenate(
                [jnp.zeros((HEAD, HEAD), jnp.float32), cache_ref[0, head].astype(jnp.float32)], axis=1
            )

    for head in range(heads):
        rows = slice(head * BLOCK, (head + 1) * BLOCK)
        state = total[head]
        fixed = (
            jnp.concatenate([jnp.zeros((BLOCK, HEAD), jnp.float32), values_ref[0, rows, :]], axis=1)
            - fine(weighted_ref[0, rows, :], state)
        )
        last = col_ref[0, 4:5, head * BLOCK : head * BLOCK + 1]
        total[head] = last * state + fine(key_ref[0, rows, :], fixed, ((0,), (0,)))

    @pl.when(block == pl.num_programs(0) - 1)
    def _():
        out_ref[...] = total[...].astype(jnp.bfloat16)


def enter_kernel(maps_ref, out_ref, state):
    @pl.when(pl.program_id(0) == 0)
    def _():
        state[...] = jnp.zeros_like(state)

    for head in range(state.shape[0]):
        both = maps_ref[0, head]
        out_ref[0, head] = state[head].astype(jnp.bfloat16)
        high, low = split(state[head])
        contract = ((1,), (0,))
        state[head] = (
            product(both[:, :HEAD], high, contract)
            + product(both[:, :HEAD], low, contract)
            + both[:, HEAD:].astype(jnp.float32)
        )


def enter_states(maps):
    shards, heads = maps.shape[:2]
    return pl.pallas_call(
        enter_kernel,
        grid=(shards,),
        in_specs=[pl.BlockSpec((1, heads, HEAD, 2 * HEAD), lambda step: (step, 0, 0, 0))],
        out_specs=pl.BlockSpec((1, heads, HEAD, HEAD), lambda step: (step, 0, 0, 0)),
        out_shape=jax.ShapeDtypeStruct((shards, heads, HEAD, HEAD), jnp.bfloat16),
        scratch_shapes=[pltpu.VMEM((heads, HEAD, HEAD), jnp.float32)],
    )(maps)


def advance_kernel(
    first_ref, slot_ref,
    maps_ref, query_ref, key_ref, weighted_ref, values_ref, mix_ref, col_ref, cache_ref, z_ref, gain_ref,
    out_ref, total,
):
    block = pl.program_id(0)
    heads = total.shape[0]

    @pl.when(block == 0)
    def _():
        total[...] = maps_ref[...].astype(jnp.float32)

    @pl.when(first_ref[block] == 1)
    def _():
        for head in range(heads):
            total[head] = cache_ref[0, head].astype(jnp.float32)

    for pack in range(heads // PACK):
        fixed_rows, outputs = [], []
        for inner in range(PACK):
            head = pack * PACK + inner
            rows = slice(head * BLOCK, (head + 1) * BLOCK)
            state = total[head]
            fixed = values_ref[0, rows, :] - fine(weighted_ref[0, rows, :], state)
            outputs.append(product(query_ref[0, rows, :], state.astype(jnp.bfloat16), ((1,), (0,))))
            last = col_ref[0, 4:5, head * BLOCK : head * BLOCK + 1]
            total[head] = last * state + fine(key_ref[0, rows, :], fixed, ((0,), (0,)))
            fixed_rows.append(fixed.astype(jnp.bfloat16))
        rows = slice(pack * LANES, (pack + 1) * LANES)
        core = jnp.concatenate(outputs, axis=0) + product(
            mix_ref[0, rows, :], jnp.concatenate(fixed_rows, axis=0), ((1,), (0,))
        )
        core = core * lax.rsqrt(jnp.mean(core * core, axis=1, keepdims=True) + 1e-06) * gain_ref[...]
        for inner in range(PACK):
            columns = slice((pack * PACK + inner) * HEAD, (pack * PACK + inner + 1) * HEAD)
            gate = silu(z_ref[:, columns].astype(jnp.float32))
            out_ref[:, columns] = (core[inner * BLOCK : (inner + 1) * BLOCK] * gate).astype(jnp.bfloat16)


def expert_apply(arrived, expert_gate, expert_up, expert_down):
    flat_rows = arrived.reshape(-1, D)
    gate_part = jnp.dot(flat_rows, expert_gate[0], preferred_element_type=jnp.float32)
    up_part = jnp.dot(flat_rows, expert_up[0], preferred_element_type=jnp.float32)
    hidden = (jax.nn.silu(gate_part) * up_part).astype(jnp.bfloat16)
    result = jnp.dot(hidden, expert_down[0], preferred_element_type=jnp.float32).astype(
        jnp.bfloat16
    )
    return result.reshape(arrived.shape)


def local(
    qkv_input,
    z_gate,
    beta_logit,
    decay_input,
    decay_rate,
    conv_weight,
    cache_state,
    cache_tail,
    block_request,
    cache_owner,
    norm_gain,
    out_weight,
    residual,
    post_gain,
    expert_ids,
    expert_weights,
    expert_gate,
    expert_up,
    expert_down,
):
    seq_len, key_heads, row_width = qkv_input.shape
    blocks = seq_len // BLOCK
    head_count = z_gate.shape[1] // HEAD
    seq_count = lax.axis_size("seq")
    exp_count = lax.axis_size("exp")
    previous = jnp.concatenate([jnp.full((1,), -1, jnp.int32), block_request[:-1]])
    starts_all = block_request != previous
    first_block = lax.axis_index("seq") * blocks
    local_request = lax.dynamic_slice_in_dim(block_request, first_block, blocks, 0)
    local_start = lax.dynamic_slice_in_dim(starts_all, first_block, blocks, 0)
    request_ids = jnp.arange(cache_owner.shape[0], dtype=jnp.int32)
    local_slot = jnp.sum(
        jnp.where(local_request[:, None] == request_ids[None, :], cache_owner[None, :], 0), axis=1
    )
    states_all = lax.all_gather(cache_state.astype(jnp.bfloat16), "seq", axis=0, tiled=True)
    width = key_heads * row_width
    rows_flat = qkv_input.reshape(seq_len, width)
    edge = jnp.concatenate(
        [
            cache_tail.astype(jnp.bfloat16).reshape(-1, width),
            rows_flat[seq_len - (CONV - 1) :],
        ],
        axis=0,
    )
    edges = lax.all_to_all(
        jnp.broadcast_to(edge[None], (seq_count,) + edge.shape), "seq", 0, 0, tiled=True
    )
    tails_all = edges[:, : -(CONV - 1)].reshape(-1, CONV - 1, width)
    place = lax.axis_index("seq")
    rim_rows = lax.dynamic_index_in_dim(
        edges[:, -(CONV - 1) :], jnp.maximum(place - 1, 0), 0, False
    )
    before = jnp.concatenate(
        [rim_rows[None], rows_flat.reshape(blocks, BLOCK, width)[:-1, BLOCK - (CONV - 1) :]], axis=0
    )
    before = jnp.where(local_start[:, None, None], tails_all[local_slot], before)
    before = jnp.pad(before.astype(jnp.float32), ((0, 0), (8 - (CONV - 1), 0), (0, 0)))
    beta = jax.nn.sigmoid(beta_logit).reshape(blocks, BLOCK, head_count).transpose(0, 2, 1)
    log_decay = (
        (-decay_rate[None, :] * jax.nn.softplus(decay_input))
        .reshape(blocks, BLOCK, head_count)
        .transpose(0, 2, 1)
    )
    running = jnp.cumsum(log_decay, axis=-1)
    last = running[..., -1:]
    grown = jnp.exp(last)
    columns = jnp.stack(
        [running, beta, jnp.exp(running), jnp.exp(last - running)]
        + [jnp.broadcast_to(grown, running.shape)] * 4,
        axis=1,
    ).reshape(blocks, 8, head_count * BLOCK)
    packs = head_count // PACK
    stacked = head_count * BLOCK
    rows_spec = pl.BlockSpec((1, stacked, HEAD), lambda b, *_: (b, 0, 0))
    mix_spec = pl.BlockSpec((1, stacked, LANES), lambda b, *_: (b, 0, 0))
    col_spec = pl.BlockSpec((1, 8, stacked), lambda b, *_: (b, 0, 0))
    cache_spec = pl.BlockSpec(
        (1, head_count, HEAD, HEAD), lambda b, first, slot, *_: (slot[b], 0, 0, 0)
    )
    params = pltpu.CompilerParams(vmem_limit_bytes=VMEM_LIMIT)
    rows_shape = (blocks, stacked, HEAD)
    queries, carried, weighted, new_values, mix = pl.pallas_call(
        parts_kernel,
        grid=(blocks,),
        in_specs=[
            pl.BlockSpec((BLOCK, width), lambda b: (b, 0)),
            pl.BlockSpec((1, 8, width), lambda b: (b, 0, 0)),
            pl.BlockSpec((CONV, width), lambda b: (0, 0)),
            col_spec,
        ],
        out_specs=[rows_spec] * 4 + [mix_spec],
        out_shape=[
            jax.ShapeDtypeStruct(rows_shape, jnp.bfloat16),
            jax.ShapeDtypeStruct(rows_shape, jnp.float32),
            jax.ShapeDtypeStruct(rows_shape, jnp.float32),
            jax.ShapeDtypeStruct(rows_shape, jnp.float32),
            jax.ShapeDtypeStruct((blocks, stacked, LANES), jnp.bfloat16),
        ],
        scratch_shapes=[pltpu.VMEM((8 + BLOCK, width), jnp.float32)],
        compiler_params=params,
        cost_estimate=pl.CostEstimate(
            flops=blocks * packs * 40 * 2 * LANES**3, bytes_accessed=16 * 2**20, transcendentals=0
        ),
    )(rows_flat, before, conv_weight.reshape(CONV, width), columns)
    firsts = local_start.astype(jnp.int32)
    own_map = pl.pallas_call(
        maps_kernel,
        grid_spec=pltpu.PrefetchScalarGridSpec(
            num_scalar_prefetch=2,
            grid=(blocks,),
            in_specs=[rows_spec, rows_spec, rows_spec, col_spec, cache_spec],
            out_specs=pl.BlockSpec((head_count, HEAD, 2 * HEAD), lambda b, *_: (0, 0, 0)),
            scratch_shapes=[pltpu.VMEM((head_count, HEAD, 2 * HEAD), jnp.float32)],
        ),
        out_shape=jax.ShapeDtypeStruct((head_count, HEAD, 2 * HEAD), jnp.bfloat16),
        compiler_params=params,
    )(firsts, local_slot, carried, weighted, new_values, columns, states_all)
    if head_count % seq_count == 0:
        swapped = lax.all_to_all(own_map, "seq", 0, 0, tiled=True)
        incoming = lax.all_to_all(
            enter_states(swapped.reshape(seq_count, -1, HEAD, 2 * HEAD)).reshape(
                head_count, HEAD, HEAD
            ),
            "seq",
            0,
            0,
            tiled=True,
        )
    else:
        incoming = lax.dynamic_index_in_dim(
            enter_states(lax.all_gather(own_map, "seq")), place, 0, False
        )
    gated = pl.pallas_call(
        advance_kernel,
        grid_spec=pltpu.PrefetchScalarGridSpec(
            num_scalar_prefetch=2,
            grid=(blocks,),
            in_specs=[
                pl.BlockSpec((head_count, HEAD, HEAD), lambda b, *_: (0, 0, 0)),
                rows_spec,
                rows_spec,
                rows_spec,
                rows_spec,
                mix_spec,
                col_spec,
                cache_spec,
                pl.BlockSpec((BLOCK, head_count * HEAD), lambda b, *_: (b, 0)),
                pl.BlockSpec((1, HEAD), lambda b, *_: (0, 0)),
            ],
            out_specs=pl.BlockSpec((BLOCK, head_count * HEAD), lambda b, *_: (b, 0)),
            scratch_shapes=[pltpu.VMEM((head_count, HEAD, HEAD), jnp.float32)],
        ),
        out_shape=jax.ShapeDtypeStruct(z_gate.shape, jnp.bfloat16),
        compiler_params=params,
    )(
        firsts, local_slot,
        incoming, queries, carried, weighted, new_values, mix, columns, states_all, z_gate, norm_gain[None],
    )
    rows_in = gated
    attn = lax.psum_scatter(
        jnp.dot(rows_in, out_weight, preferred_element_type=jnp.float32).astype(jnp.bfloat16),
        "exp",
        scatter_dimension=0,
        tiled=True,
    ).astype(jnp.float32)
    mid_wide = (residual.astype(jnp.float32) + attn).astype(jnp.bfloat16).astype(jnp.float32)
    normed = (
        mid_wide
        * lax.rsqrt(jnp.mean(mid_wide * mid_wide, axis=-1, keepdims=True) + 1e-06)
        * post_gain
    ).astype(jnp.bfloat16)
    route = expert_weights / jnp.sum(expert_weights, axis=-1, keepdims=True)
    token_count, top_count = expert_ids.shape
    expert_count = seq_count * exp_count
    capacity = max(2, token_count * top_count * 6 // (expert_count * 5))
    names = jnp.arange(expert_count, dtype=expert_ids.dtype)
    chosen = expert_ids[:, :, None] == names
    hot = jnp.any(chosen, axis=1)
    share = jnp.sum(jnp.where(chosen, route[:, :, None], 0.0), axis=1)
    rank = jnp.cumsum(hot.astype(jnp.int32), axis=0) - 1
    placed = hot[:, :, None] & (rank[:, :, None] == jnp.arange(capacity, dtype=jnp.int32))
    flat_placed = placed.astype(jnp.bfloat16).reshape(token_count, expert_count * capacity)
    outgoing = jnp.dot(flat_placed.T, normed, preferred_element_type=jnp.float32).astype(jnp.bfloat16)
    devices = ("seq", "exp")
    arrived = lax.all_to_all(outgoing, devices, split_axis=0, concat_axis=0, tiled=True)
    results = expert_apply(arrived, expert_gate, expert_up, expert_down)
    returned = lax.all_to_all(results, devices, split_axis=0, concat_axis=0, tiled=True)
    share_high, share_low = split(share)
    moe_sum = sum(
        jnp.dot(
            (placed * part[:, :, None]).reshape(token_count, expert_count * capacity),
            returned,
            preferred_element_type=jnp.float32,
        )
        for part in (share_high, share_low)
    )
    return (mid_wide + moe_sum).astype(jnp.bfloat16)


def solution(mesh):
    in_specs = (
        P("seq", "exp", None),
        P("seq", "exp"),
        P("seq", "exp"),
        P("seq", "exp"),
        P("exp"),
        P(None, "exp", None),
        P("seq", "exp", None, None),
        P("seq", None, "exp", None),
        P(),
        P(),
        P(),
        P("exp", None),
        P(("seq", "exp"), None),
        P(),
        P(("seq", "exp"), None),
        P(("seq", "exp"), None),
        P(("seq", "exp"), None, None),
        P(("seq", "exp"), None, None),
        P(("seq", "exp"), None, None),
    )
    out_specs = P(("seq", "exp"), None)
    return jax.shard_map(local, mesh=mesh, in_specs=in_specs, out_specs=out_specs, check_vma=False)
```

```python
import math

import jax
import jax.numpy as jnp
from jax import lax
from jax.experimental import pallas as pl
from jax.experimental.pallas import tpu as pltpu
from jax.sharding import PartitionSpec as P

D = 2048
HEAD = 128
GROUP = 2
CONV = 4
BLOCK = 64


PACK = 2
LANES = PACK * BLOCK
VMEM_LIMIT = 56 * 1024 * 1024


def product(left, right, contract):
    return lax.dot_general(left, right, (contract, ((), ())), preferred_element_type=jnp.float32)


def split(value):
    high = value.astype(jnp.bfloat16)
    return (high, (value - high.astype(jnp.float32)).astype(jnp.bfloat16))


def fine(left, right, contract=((1,), (0,))):
    left_high, left_low = split(left)
    right_high, right_low = split(right)
    return (
        product(left_high, right_high, contract)
        + product(left_high, right_low, contract)
        + product(left_low, right_high, contract)
    )


def fine_halves(left, right):
    left_high, left_low = left
    right_high, right_low = right
    contract = ((1,), (0,))
    return product(
        jnp.concatenate([left_high, left_low], axis=1),
        jnp.concatenate([right_high, right_high], axis=0),
        contract,
    ) + product(left_high, right_low, contract)


def coarse(left, right, contract=((1,), (0,))):
    return product(left.astype(jnp.bfloat16), right.astype(jnp.bfloat16), contract)


def silu(value):
    return value / (1.0 + jnp.exp(-value))


def parts_kernel(
    x_ref, before_ref, taps_ref, row_ref, query_ref, key_ref, weighted_ref, values_ref, mix_ref, ext
):
    ext[0:8, :] = before_ref[0]
    ext[8:, :] = x_ref[...].astype(jnp.float32)
    row_id = lax.broadcasted_iota(jnp.int32, (LANES, LANES), 0)
    col_id = lax.broadcasted_iota(jnp.int32, (LANES, LANES), 1)
    same_head = row_id // BLOCK == col_id // BLOCK
    inclusive = same_head & (row_id >= col_id)
    strict = same_head & (row_id > col_id)
    group_width = (2 + GROUP) * HEAD
    heads = row_ref.shape[2] // BLOCK
    cols = row_ref[0].T
    lowers, sides = [], []
    for pack in range(heads // PACK):
        queries, keys, values = [], [], []
        for group in range(PACK // GROUP):
            first = (pack * (PACK // GROUP) + group) * group_width
            columns = slice(first, first + group_width)
            mixed = ext[5 : 5 + BLOCK, columns] * taps_ref[0:1, columns]
            for tap in range(1, CONV):
                mixed = mixed + ext[5 + tap : 5 + tap + BLOCK, columns] * taps_ref[tap : tap + 1, columns]
            mixed = silu(mixed)
            query = mixed[:, :HEAD]
            query = query * (
                lax.rsqrt(jnp.sum(query * query, axis=1, keepdims=True) + 1e-06) / math.sqrt(HEAD)
            )
            key = mixed[:, HEAD : 2 * HEAD]
            key = key * lax.rsqrt(jnp.sum(key * key, axis=1, keepdims=True) + 1e-06)
            queries += [query, query]
            keys += [key, key]
            values += [mixed[:, 2 * HEAD : 3 * HEAD], mixed[:, 3 * HEAD :]]
        query = jnp.concatenate(queries, axis=0)
        key = jnp.concatenate(keys, axis=0)
        value = jnp.concatenate(values, axis=0)
        rows = slice(pack * LANES, (pack + 1) * LANES)
        col = cols[rows, :]
        running, beta, growth, tail = col[:, 0:1], col[:, 1:2], col[:, 2:3], col[:, 3:4]
        decay = jnp.where(
            inclusive, jnp.exp(jnp.where(inclusive, running - row_ref[0, 0:1, rows], 0.0)), 0.0
        )
        across = ((1,), (1,))
        lower = jnp.where(strict, beta * fine(key, key, across) * decay, 0.0)
        mix_ref[0, rows, :] = (coarse(query, key, across) * decay).astype(jnp.bfloat16)
        query_ref[0, rows, :] = (growth * query).astype(jnp.bfloat16)
        key_ref[0, rows, :] = tail * key
        lowers.append(lower)
        sides.append(jnp.concatenate([(beta * growth) * key, beta * value], axis=1))
    unit = jnp.where(row_id == col_id, 1.0, 0.0)
    pairs = row_id // 2 == col_id // 2
    inverses = [unit - jnp.where(pairs, lower, 0.0) for lower in lowers]
    size = 2
    while size < BLOCK:
        joint = (row_id // (2 * size) == col_id // (2 * size)) & (row_id // size != col_id // size)
        halves = [split(inverse) for inverse in inverses]
        between = [split(jnp.where(joint, lower, 0.0)) for lower in lowers]
        steps = [fine_halves(half, mid) for half, mid in zip(halves, between)]
        steps = [split(step) for step in steps]
        steps = [fine_halves(step, half) for step, half in zip(steps, halves)]
        inverses = [inverse - step for inverse, step in zip(inverses, steps)]
        size *= 2
    solved = [fine_halves(split(inverse), split(side)) for inverse, side in zip(inverses, sides)]
    for pack, one in enumerate(solved):
        rows = slice(pack * LANES, (pack + 1) * LANES)
        weighted_ref[0, rows, :] = one[:, :HEAD]
        values_ref[0, rows, :] = one[:, HEAD:]


def maps_kernel(first_ref, slot_ref, key_ref, weighted_ref, values_ref, col_ref, cache_ref, out_ref, total):
    block = pl.program_id(0)
    heads = total.shape[0]

    @pl.when(block == 0)
    def _():
        eye = jnp.where(
            lax.broadcasted_iota(jnp.int32, (HEAD, HEAD), 0)
            == lax.broadcasted_iota(jnp.int32, (HEAD, HEAD), 1),
            1.0,
            0.0,
        )
        for head in range(heads):
            total[head] = jnp.concatenate([eye, jnp.zeros((HEAD, HEAD), jnp.float32)], axis=1)

    @pl.when(first_ref[block] == 1)
    def _():
        for head in range(heads):
            total[head] = jnp.concatenate(
                [jnp.zeros((HEAD, HEAD), jnp.float32), cache_ref[0, head].astype(jnp.float32)], axis=1
            )

    spans = [slice(head * BLOCK, (head + 1) * BLOCK) for head in range(heads)]
    states = [total[head] for head in range(heads)]
    blank = jnp.zeros((BLOCK, HEAD), jnp.float32)
    moved = [
        fine_halves(split(weighted_ref[0, rows, :]), split(state)) for rows, state in zip(spans, states)
    ]
    fixed = [
        jnp.concatenate([blank, values_ref[0, rows, :]], axis=1) - move
        for rows, move in zip(spans, moved)
    ]
    added = [
        fine(key_ref[0, rows, :], part, ((0,), (0,))) for rows, part in zip(spans, fixed)
    ]
    for head in range(heads):
        last = col_ref[0, 4:5, head * BLOCK : head * BLOCK + 1]
        total[head] = last * states[head] + added[head]

    @pl.when(block == pl.num_programs(0) - 1)
    def _():
        out_ref[...] = total[...].astype(jnp.bfloat16)


def enter_kernel(maps_ref, out_ref, state):
    @pl.when(pl.program_id(0) == 0)
    def _():
        state[...] = jnp.zeros_like(state)

    for head in range(state.shape[0]):
        both = maps_ref[0, head]
        out_ref[0, head] = state[head].astype(jnp.bfloat16)
        high, low = split(state[head])
        contract = ((1,), (0,))
        state[head] = (
            product(both[:, :HEAD], high, contract)
            + product(both[:, :HEAD], low, contract)
            + both[:, HEAD:].astype(jnp.float32)
        )


def enter_states(maps):
    shards, heads = maps.shape[:2]
    return pl.pallas_call(
        enter_kernel,
        grid=(shards,),
        in_specs=[pl.BlockSpec((1, heads, HEAD, 2 * HEAD), lambda step: (step, 0, 0, 0))],
        out_specs=pl.BlockSpec((1, heads, HEAD, HEAD), lambda step: (step, 0, 0, 0)),
        out_shape=jax.ShapeDtypeStruct((shards, heads, HEAD, HEAD), jnp.bfloat16),
        scratch_shapes=[pltpu.VMEM((heads, HEAD, HEAD), jnp.float32)],
    )(maps)


def advance_kernel(
    first_ref, slot_ref,
    maps_ref, query_ref, key_ref, weighted_ref, values_ref, mix_ref, col_ref, cache_ref, z_ref, gain_ref,
    out_ref, total,
):
    block = pl.program_id(0)
    heads = total.shape[0]

    @pl.when(block == 0)
    def _():
        total[...] = maps_ref[...].astype(jnp.float32)

    @pl.when(first_ref[block] == 1)
    def _():
        for head in range(heads):
            total[head] = cache_ref[0, head].astype(jnp.float32)

    spans = [slice(head * BLOCK, (head + 1) * BLOCK) for head in range(heads)]
    states = [total[head] for head in range(heads)]
    halves = [split(state) for state in states]
    moved = [
        fine_halves(split(weighted_ref[0, rows, :]), half) for rows, half in zip(spans, halves)
    ]
    outputs = [
        product(query_ref[0, rows, :], half[0], ((1,), (0,))) for rows, half in zip(spans, halves)
    ]
    fixed = [values_ref[0, rows, :] - move for rows, move in zip(spans, moved)]
    added = [
        fine(key_ref[0, rows, :], part, ((0,), (0,))) for rows, part in zip(spans, fixed)
    ]
    for head in range(heads):
        last = col_ref[0, 4:5, head * BLOCK : head * BLOCK + 1]
        total[head] = last * states[head] + added[head]
    fixed = [part.astype(jnp.bfloat16) for part in fixed]
    for pack in range(heads // PACK):
        rows = slice(pack * LANES, (pack + 1) * LANES)
        members = slice(pack * PACK, (pack + 1) * PACK)
        core = jnp.concatenate(outputs[members], axis=0) + product(
            mix_ref[0, rows, :], jnp.concatenate(fixed[members], axis=0), ((1,), (0,))
        )
        core = core * lax.rsqrt(jnp.mean(core * core, axis=1, keepdims=True) + 1e-06) * gain_ref[...]
        for inner in range(PACK):
            columns = slice((pack * PACK + inner) * HEAD, (pack * PACK + inner + 1) * HEAD)
            gate = silu(z_ref[:, columns].astype(jnp.float32))
            out_ref[:, columns] = (core[inner * BLOCK : (inner + 1) * BLOCK] * gate).astype(jnp.bfloat16)


def expert_apply(arrived, expert_gate, expert_up, expert_down):
    flat_rows = arrived.reshape(-1, D)
    gate_part = jnp.dot(flat_rows, expert_gate[0], preferred_element_type=jnp.float32)
    up_part = jnp.dot(flat_rows, expert_up[0], preferred_element_type=jnp.float32)
    hidden = (jax.nn.silu(gate_part) * up_part).astype(jnp.bfloat16)
    result = jnp.dot(hidden, expert_down[0], preferred_element_type=jnp.float32).astype(
        jnp.bfloat16
    )
    return result.reshape(arrived.shape)


def local(
    qkv_input,
    z_gate,
    beta_logit,
    decay_input,
    decay_rate,
    conv_weight,
    cache_state,
    cache_tail,
    block_request,
    cache_owner,
    norm_gain,
    out_weight,
    residual,
    post_gain,
    expert_ids,
    expert_weights,
    expert_gate,
    expert_up,
    expert_down,
):
    seq_len, key_heads, row_width = qkv_input.shape
    blocks = seq_len // BLOCK
    head_count = z_gate.shape[1] // HEAD
    seq_count = lax.axis_size("seq")
    exp_count = lax.axis_size("exp")
    previous = jnp.concatenate([jnp.full((1,), -1, jnp.int32), block_request[:-1]])
    starts_all = block_request != previous
    first_block = lax.axis_index("seq") * blocks
    local_request = lax.dynamic_slice_in_dim(block_request, first_block, blocks, 0)
    local_start = lax.dynamic_slice_in_dim(starts_all, first_block, blocks, 0)
    request_ids = jnp.arange(cache_owner.shape[0], dtype=jnp.int32)
    local_slot = jnp.sum(
        jnp.where(local_request[:, None] == request_ids[None, :], cache_owner[None, :], 0), axis=1
    )
    states_all = lax.all_gather(cache_state.astype(jnp.bfloat16), "seq", axis=0, tiled=True)
    width = key_heads * row_width
    rows_flat = qkv_input.reshape(seq_len, width)
    edge = jnp.concatenate(
        [
            cache_tail.astype(jnp.bfloat16).reshape(-1, width),
            rows_flat[seq_len - (CONV - 1) :],
        ],
        axis=0,
    )
    edges = lax.all_to_all(
        jnp.broadcast_to(edge[None], (seq_count,) + edge.shape), "seq", 0, 0, tiled=True
    )
    tails_all = edges[:, : -(CONV - 1)].reshape(-1, CONV - 1, width)
    place = lax.axis_index("seq")
    rim_rows = lax.dynamic_index_in_dim(
        edges[:, -(CONV - 1) :], jnp.maximum(place - 1, 0), 0, False
    )
    before = jnp.concatenate(
        [rim_rows[None], rows_flat.reshape(blocks, BLOCK, width)[:-1, BLOCK - (CONV - 1) :]], axis=0
    )
    before = jnp.where(local_start[:, None, None], tails_all[local_slot], before)
    before = jnp.pad(before.astype(jnp.float32), ((0, 0), (8 - (CONV - 1), 0), (0, 0)))
    beta = jax.nn.sigmoid(beta_logit).reshape(blocks, BLOCK, head_count).transpose(0, 2, 1)
    log_decay = (
        (-decay_rate[None, :] * jax.nn.softplus(decay_input))
        .reshape(blocks, BLOCK, head_count)
        .transpose(0, 2, 1)
    )
    running = jnp.cumsum(log_decay, axis=-1)
    last = running[..., -1:]
    grown = jnp.exp(last)
    columns = jnp.stack(
        [running, beta, jnp.exp(running), jnp.exp(last - running)]
        + [jnp.broadcast_to(grown, running.shape)] * 4,
        axis=1,
    ).reshape(blocks, 8, head_count * BLOCK)
    packs = head_count // PACK
    stacked = head_count * BLOCK
    rows_spec = pl.BlockSpec((1, stacked, HEAD), lambda b, *_: (b, 0, 0))
    mix_spec = pl.BlockSpec((1, stacked, LANES), lambda b, *_: (b, 0, 0))
    col_spec = pl.BlockSpec((1, 8, stacked), lambda b, *_: (b, 0, 0))
    cache_spec = pl.BlockSpec(
        (1, head_count, HEAD, HEAD), lambda b, first, slot, *_: (slot[b], 0, 0, 0)
    )
    params = pltpu.CompilerParams(vmem_limit_bytes=VMEM_LIMIT)
    rows_shape = (blocks, stacked, HEAD)
    queries, carried, weighted, new_values, mix = pl.pallas_call(
        parts_kernel,
        grid=(blocks,),
        in_specs=[
            pl.BlockSpec((BLOCK, width), lambda b: (b, 0)),
            pl.BlockSpec((1, 8, width), lambda b: (b, 0, 0)),
            pl.BlockSpec((CONV, width), lambda b: (0, 0)),
            col_spec,
        ],
        out_specs=[rows_spec] * 4 + [mix_spec],
        out_shape=[
            jax.ShapeDtypeStruct(rows_shape, jnp.bfloat16),
            jax.ShapeDtypeStruct(rows_shape, jnp.float32),
            jax.ShapeDtypeStruct(rows_shape, jnp.float32),
            jax.ShapeDtypeStruct(rows_shape, jnp.float32),
            jax.ShapeDtypeStruct((blocks, stacked, LANES), jnp.bfloat16),
        ],
        scratch_shapes=[pltpu.VMEM((8 + BLOCK, width), jnp.float32)],
        compiler_params=params,
        cost_estimate=pl.CostEstimate(
            flops=blocks * packs * 40 * 2 * LANES**3, bytes_accessed=16 * 2**20, transcendentals=0
        ),
    )(rows_flat, before, conv_weight.reshape(CONV, width), columns)
    firsts = local_start.astype(jnp.int32)
    own_map = pl.pallas_call(
        maps_kernel,
        grid_spec=pltpu.PrefetchScalarGridSpec(
            num_scalar_prefetch=2,
            grid=(blocks,),
            in_specs=[rows_spec, rows_spec, rows_spec, col_spec, cache_spec],
            out_specs=pl.BlockSpec((head_count, HEAD, 2 * HEAD), lambda b, *_: (0, 0, 0)),
            scratch_shapes=[pltpu.VMEM((head_count, HEAD, 2 * HEAD), jnp.float32)],
        ),
        out_shape=jax.ShapeDtypeStruct((head_count, HEAD, 2 * HEAD), jnp.bfloat16),
        compiler_params=params,
    )(firsts, local_slot, carried, weighted, new_values, columns, states_all)
    if head_count % seq_count == 0:
        swapped = lax.all_to_all(own_map, "seq", 0, 0, tiled=True)
        incoming = lax.all_to_all(
            enter_states(swapped.reshape(seq_count, -1, HEAD, 2 * HEAD)).reshape(
                head_count, HEAD, HEAD
            ),
            "seq",
            0,
            0,
            tiled=True,
        )
    else:
        incoming = lax.dynamic_index_in_dim(
            enter_states(lax.all_gather(own_map, "seq")), place, 0, False
        )
    gated = pl.pallas_call(
        advance_kernel,
        grid_spec=pltpu.PrefetchScalarGridSpec(
            num_scalar_prefetch=2,
            grid=(blocks,),
            in_specs=[
                pl.BlockSpec((head_count, HEAD, HEAD), lambda b, *_: (0, 0, 0)),
                rows_spec,
                rows_spec,
                rows_spec,
                rows_spec,
                mix_spec,
                col_spec,
                cache_spec,
                pl.BlockSpec((BLOCK, head_count * HEAD), lambda b, *_: (b, 0)),
                pl.BlockSpec((1, HEAD), lambda b, *_: (0, 0)),
            ],
            out_specs=pl.BlockSpec((BLOCK, head_count * HEAD), lambda b, *_: (b, 0)),
            scratch_shapes=[pltpu.VMEM((head_count, HEAD, HEAD), jnp.float32)],
        ),
        out_shape=jax.ShapeDtypeStruct(z_gate.shape, jnp.bfloat16),
        compiler_params=params,
    )(
        firsts, local_slot,
        incoming, queries, carried, weighted, new_values, mix, columns, states_all, z_gate, norm_gain[None],
    )
    rows_in = gated
    attn = lax.psum_scatter(
        jnp.dot(rows_in, out_weight, preferred_element_type=jnp.float32).astype(jnp.bfloat16),
        "exp",
        scatter_dimension=0,
        tiled=True,
    ).astype(jnp.float32)
    mid_wide = (residual.astype(jnp.float32) + attn).astype(jnp.bfloat16).astype(jnp.float32)
    normed = (
        mid_wide
        * lax.rsqrt(jnp.mean(mid_wide * mid_wide, axis=-1, keepdims=True) + 1e-06)
        * post_gain
    ).astype(jnp.bfloat16)
    route = expert_weights / jnp.sum(expert_weights, axis=-1, keepdims=True)
    token_count, top_count = expert_ids.shape
    expert_count = seq_count * exp_count
    capacity = max(2, token_count * top_count * 6 // (expert_count * 5))
    names = jnp.arange(expert_count, dtype=expert_ids.dtype)
    chosen = expert_ids[:, :, None] == names
    hot = jnp.any(chosen, axis=1)
    share = jnp.sum(jnp.where(chosen, route[:, :, None], 0.0), axis=1)
    rank = jnp.cumsum(hot.astype(jnp.int32), axis=0) - 1
    placed = hot[:, :, None] & (rank[:, :, None] == jnp.arange(capacity, dtype=jnp.int32))
    flat_placed = placed.astype(jnp.bfloat16).reshape(token_count, expert_count * capacity)
    outgoing = jnp.dot(flat_placed.T, normed, preferred_element_type=jnp.float32).astype(jnp.bfloat16)
    devices = ("seq", "exp")
    arrived = lax.all_to_all(outgoing, devices, split_axis=0, concat_axis=0, tiled=True)
    results = expert_apply(arrived, expert_gate, expert_up, expert_down)
    returned = lax.all_to_all(results, devices, split_axis=0, concat_axis=0, tiled=True)
    share_high, share_low = split(share)
    moe_sum = sum(
        jnp.dot(
            (placed * part[:, :, None]).reshape(token_count, expert_count * capacity),
            returned,
            preferred_element_type=jnp.float32,
        )
        for part in (share_high, share_low)
    )
    return (mid_wide + moe_sum).astype(jnp.bfloat16)


def solution(mesh):
    in_specs = (
        P("seq", "exp", None),
        P("seq", "exp"),
        P("seq", "exp"),
        P("seq", "exp"),
        P("exp"),
        P(None, "exp", None),
        P("seq", "exp", None, None),
        P("seq", None, "exp", None),
        P(),
        P(),
        P(),
        P("exp", None),
        P(("seq", "exp"), None),
        P(),
        P(("seq", "exp"), None),
        P(("seq", "exp"), None),
        P(("seq", "exp"), None, None),
        P(("seq", "exp"), None, None),
        P(("seq", "exp"), None, None),
    )
    out_specs = P(("seq", "exp"), None)
    return jax.shard_map(local, mesh=mesh, in_specs=in_specs, out_specs=out_specs, check_vma=False)
```
